32 devices in a mesh: inst: 8 (over z, x), head: 4 (over y, core).
Axes of the slice: x: 2, y: 2, z: 4, core: 2. Of those that a mesh axis runs over, the one named last changes fastest.
Arguments:
- cache_keys: bfloat16 [1024, 64, 8, 128], P('inst', None, 'head'), may hold values from -10 to 10
- cache_values: bfloat16 [1024, 64, 8, 128], P('inst', None, 'head'), may hold values from -6 to 6
- slot_req: int32 [1024], P('inst'), may hold values from 0 to 11, as said below
- slot_fill: int32 [1024], P('inst'), may hold values from 0 to 64, as said below
- mig_src: int32 [8, 8, 2], P('inst'), may hold values from -1 to 127, as said below
- mig_dst: int32 [8, 8, 2], P('inst'), may hold values from -1 to 71, as said below
- queries: bfloat16 [16, 12, 128, 128], P(None, None, 'head'), may hold values from -64 to 64
- new_keys: bfloat16 [16, 12, 8, 128], P(None, None, 'head'), may hold values from -10 to 10
- new_values: bfloat16 [16, 12, 8, 128], P(None, None, 'head'), may hold values from -6 to 6
- out_weight: bfloat16 [16384, 16384], P('head', 'inst'), may hold values from -0.046875 to 0.046875
Outputs:
- moved_keys: bfloat16 [1024, 64, 8, 128], P('inst', None, 'head')
- moved_values: bfloat16 [1024, 64, 8, 128], P('inst', None, 'head')
- output: bfloat16 [16, 12, 16384], P(None, None, ('inst', 'head'))
The draws below stay inside these ranges and needn't reach their ends.
Inputs may be any that keep to these rules, and one draw needn't show every extreme that they name: `slot_req`: request of each slot; requests hold very different numbers of pages. A slot's live tokens are its first slot_fill tokens; 0 means the slot is empty. Each non-negative entry names a non-empty slot of the sending instance (first index); no slot is named twice. mig_src is -1 exactly where mig_dst is -1. At most 2 pages go from one instance to another, and some pairs carry exactly 2. `mig_dst`: each non-negative entry names an empty slot of the receiving instance (second index) that is named by no other entry and is not itself a source.
All inputs are finite; a program needn't handle non-finite values.
Results may differ from the reference program's by a relative error of at most 0.0051.
Values may be sent and summed in bfloat16 or wider, within the bound.
No kernel may reach another device: no remote copies, remote signals or barrier semaphores. Data moves between devices by JAX's collectives and lax.ppermute only.
A program may use at most 256 MiB of HBM per device.

```python
import math
import jax
import jax.numpy as jnp
from jax import lax

D = 16384
HEADS = 128
KV = 8
HD = 128
PAGE = 64
SLOTS = 128
CAP = 2
REQS = 12
STEPS = 16
INSTANCES = 8


def key_base(key):
    return 2.0 * jax.random.truncated_normal(key, -5.0, 5.0, (STEPS, REQS, KV, HD), jnp.float32)


def instance_rank(key):
    return jnp.argsort(jax.random.permutation(key, INSTANCES)).astype(jnp.int32)


def slot_fill_table(key):
    rank = instance_rank(key)
    key = jax.random.fold_in(key, 5)
    heavy_rows = rank < INSTANCES // 2
    used_slots = heavy_rows[:, None] | (jnp.arange(SLOTS)[None, :] < SLOTS // 2)
    full_page = jax.random.randint(jax.random.fold_in(key, 1), (INSTANCES, SLOTS), 0, 4) < 3
    partial_value = jax.random.randint(jax.random.fold_in(key, 2), (INSTANCES, SLOTS), 1, PAGE + 1)
    fill_draw = jnp.where(full_page, PAGE, partial_value)
    return jnp.where(used_slots, fill_draw, 0).reshape(-1).astype(jnp.int32)


def slot_req_table(key):
    key = jax.random.fold_in(key, 13)
    ticket = jax.random.randint(key, (INSTANCES * SLOTS,), 0, REQS * (REQS + 1) // 2)
    bounds = jnp.arange(1, REQS) * jnp.arange(2, REQS + 1) // 2
    return jnp.sum(ticket[:, None] >= bounds[None, :], axis=1).astype(jnp.int32)


def draw_cache_keys(key, part):
    base_keys = 2.0 * jax.random.truncated_normal(jax.random.fold_in(key, 31), -5.0, 5.0, (INSTANCES * SLOTS, PAGE, KV, HD), jnp.float32)
    return base_keys.astype(jnp.bfloat16)


def draw_new_keys(key, part):
    base_keys = key_base(key)
    return base_keys.astype(jnp.bfloat16)


def draw_queries(key, part):
    key = jax.random.fold_in(key, 7)
    group_size = HEADS // KV
    query_draw = jax.random.normal(key, (STEPS, REQS, KV, group_size, HD), jnp.float32)
    return jnp.clip(query_draw, -64.0, 64.0).reshape(STEPS, REQS, HEADS, HD).astype(jnp.bfloat16)


def draw_slot_fill(key, part):
    return slot_fill_table(key)


def draw_slot_req(key, part):
    return slot_req_table(key)


def draw_mig_src(key, part):
    rank = instance_rank(key)
    key = jax.random.fold_in(key, 9)
    random_bits = jax.random.randint(key, (INSTANCES, SLOTS), 0, 2 ** 20) * SLOTS + jnp.arange(SLOTS)[None, :]
    slot_order = jnp.argsort(random_bits, axis=1).astype(jnp.int32)
    light_index = jnp.maximum(rank - INSTANCES // 2, 0)
    column = light_index[None, :, None] * CAP + jnp.arange(CAP)[None, None, :]
    source_rows = jnp.arange(INSTANCES)[:, None, None]
    chosen_slot = slot_order.reshape(-1)[source_rows * SLOTS + column]
    paired = (rank[:, None] < INSTANCES // 2) & (rank[None, :] >= INSTANCES // 2)
    return jnp.where(paired[:, :, None], chosen_slot, -1).astype(jnp.int32)


def draw_mig_dst(key, part):
    rank = instance_rank(key)
    landing = SLOTS // 2 + rank[:, None, None] * CAP + jnp.arange(CAP)[None, None, :]
    landing = jnp.broadcast_to(landing, (INSTANCES, INSTANCES, CAP))
    paired = (rank[:, None] < INSTANCES // 2) & (rank[None, :] >= INSTANCES // 2)
    return jnp.where(paired[:, :, None], landing, -1).astype(jnp.int32)


def block_scale(rng, dims, shards, low, top_value):
    loudness = 1.0
    for position, parts in shards:
        heights = jax.random.uniform(jax.random.fold_in(jax.random.fold_in(rng, 6), position), (parts,), jnp.float32, low / len(shards), top_value / len(shards))
        loudness = loudness * jnp.repeat(jnp.exp(heights), dims[position] // parts).reshape((-1,) + (1,) * (len(dims) - 1 - position))
    return loudness


def scatter_about(own_key, extent, scale, bound, shards=(), kind=jnp.bfloat16):
    values = scale * jax.random.normal(own_key, extent, jnp.float32)
    if shards:
        values = values * block_scale(own_key, extent, shards, -0.22, 0.18)
    return jnp.clip(values, -bound, bound).astype(kind)


def setup_inputs(seed: int = 0) -> dict:
    streams_of = jax.random.split(jax.random.key(seed), 11)
    cache_keys = draw_cache_keys(jax.random.fold_in(streams_of[10], 71), 0)
    cache_values = scatter_about(streams_of[1], (INSTANCES * SLOTS, PAGE, KV, HD), 1.0, 6.0, ((0, 8), (2, 4)))
    slot_req = draw_slot_req(jax.random.fold_in(streams_of[10], 71), 0)
    slot_fill = draw_slot_fill(jax.random.fold_in(streams_of[10], 71), 0)
    mig_src = draw_mig_src(jax.random.fold_in(streams_of[10], 71), 0)
    mig_dst = draw_mig_dst(jax.random.fold_in(streams_of[10], 71), 0)
    queries = draw_queries(jax.random.fold_in(streams_of[10], 71), 0)
    new_keys = draw_new_keys(jax.random.fold_in(streams_of[10], 71), 0)
    new_values = scatter_about(streams_of[8], (STEPS, REQS, KV, HD), 1.0, 6.0, ((2, 4),))
    out_weight = scatter_about(streams_of[9], (HEADS * HD, D), (HEADS * HD) ** -0.5, 0.046875, ((0, 4), (1, 8)))
    return {"cache_keys": cache_keys, "cache_values": cache_values, "slot_req": slot_req, "slot_fill": slot_fill, "mig_src": mig_src, "mig_dst": mig_dst, "queries": queries, "new_keys": new_keys, "new_values": new_values, "out_weight": out_weight}


masked_score = -1e+30

def page_scores(keys, req, fill, grouped):
    chosen = grouped[:, req].astype(jnp.float32)
    scores = jnp.einsum('snkgd,ntkd->nksgt', chosen, keys.astype(jnp.float32)) * (1.0 / math.sqrt(HD))
    live_tokens = jnp.arange(PAGE, dtype=jnp.int32)[None, :] < fill[:, None]
    live_full = live_tokens[:, None, None, None, :]
    return (jnp.where(live_full, scores, masked_score), live_full)

def fresh_scores(grouped, new_keys):
    scores = jnp.einsum('srkgd,urkd->rksgu', grouped.astype(jnp.float32), new_keys.astype(jnp.float32)) * (1.0 / math.sqrt(HD))
    causal = jnp.arange(STEPS)[None, :] <= jnp.arange(STEPS)[:, None]
    return jnp.where(causal[None, None, :, None, :], scores, masked_score)

def reference(cache_keys, cache_values, slot_req, slot_fill, mig_src, mig_dst, queries, new_keys, new_values, out_weight):
    slot_total = INSTANCES * SLOTS
    offsets = jnp.arange(INSTANCES, dtype=jnp.int32) * SLOTS
    sources = jnp.where(mig_src >= 0, mig_src + offsets[:, None, None], slot_total).reshape(-1).astype(jnp.int32)
    targets = jnp.where(mig_dst >= 0, mig_dst + offsets[None, :, None], slot_total).reshape(-1).astype(jnp.int32)
    safe_rows = jnp.minimum(sources, slot_total - 1)

    def relocate(cache_rows):
        moved_pages = cache_rows[safe_rows]
        cleared = cache_rows.at[sources].set(jnp.zeros_like(moved_pages), mode='drop')
        return cleared.at[targets].set(moved_pages, mode='drop')
    moved_keys = relocate(cache_keys)
    moved_values = relocate(cache_values)
    grouped = queries.reshape(STEPS, REQS, KV, HEADS // KV, HD)
    members = jnp.arange(REQS, dtype=jnp.int32)
    key_blocks = cache_keys.reshape(INSTANCES, SLOTS, PAGE, KV, HD)
    value_blocks = cache_values.reshape(INSTANCES, SLOTS, PAGE, KV, HD)
    req_blocks = slot_req.reshape(INSTANCES, SLOTS)
    fill_blocks = slot_fill.reshape(INSTANCES, SLOTS)
    new_part = fresh_scores(grouped, new_keys)
    fresh_peak = new_part.max(-1)

    def peak_step(running, block_item):
        keys, req, fill = block_item
        scores, _ = page_scores(keys, req, fill, grouped)
        page_peak = scores.max(-1)
        onehot = req[:, None] == members[None, :]
        block_peak = jnp.where(onehot[:, :, None, None, None], page_peak[:, None], masked_score).max(0)
        return (jnp.maximum(running, block_peak), None)
    score_peak, _ = lax.scan(peak_step, fresh_peak, (key_blocks, req_blocks, fill_blocks))

    def sum_step(running, block_item):
        keys, values, req, fill = block_item
        scores, live_full = page_scores(keys, req, fill, grouped)
        page_peak = scores.max(-1)
        weights = jnp.where(live_full, jnp.exp(scores - page_peak[..., None]), 0.0)
        weight_sum = weights.sum(-1)
        rounded = lax.optimization_barrier(weights.astype(jnp.bfloat16))
        per_slot = jnp.einsum('nksgt,ntkd->nksgd', rounded.astype(jnp.float32), values.astype(jnp.float32))
        factor = jnp.exp(page_peak - score_peak[req])
        indicator = (req[:, None] == members[None, :]).astype(jnp.float32)
        numerator = running[0] + jnp.einsum('nr,nksgd->rksgd', indicator, per_slot * factor[..., None], precision=lax.Precision.HIGHEST)
        denominator = running[1] + jnp.einsum('nr,nksg->rksg', indicator, weight_sum * factor, precision=lax.Precision.HIGHEST)
        return ((numerator, denominator), None)
    start_sums = (jnp.zeros((REQS, KV, STEPS, HEADS // KV, HD), jnp.float32), jnp.zeros((REQS, KV, STEPS, HEADS // KV), jnp.float32))
    (numerator, denominator), _ = lax.scan(sum_step, start_sums, (key_blocks, value_blocks, req_blocks, fill_blocks))
    fresh_weights = jnp.exp(new_part - fresh_peak[..., None])
    fresh_rounded = lax.optimization_barrier(fresh_weights.astype(jnp.bfloat16))
    fresh_factor = jnp.exp(fresh_peak - score_peak)
    fresh_numerator = jnp.einsum('rksgu,urkd->rksgd', fresh_rounded.astype(jnp.float32), new_values.astype(jnp.float32))
    numerator = numerator + fresh_numerator * fresh_factor[..., None]
    denominator = denominator + fresh_weights.sum(-1) * fresh_factor
    attention = (numerator / denominator[..., None]).astype(jnp.bfloat16)
    attention = attention.transpose(2, 0, 1, 3, 4).reshape(STEPS * REQS, HEADS * HD)
    output = jnp.dot(attention, out_weight, preferred_element_type=jnp.float32).astype(jnp.bfloat16).reshape(STEPS, REQS, D)
    return (moved_keys, moved_values, output)
```

```python
import functools
import math

import jax
import jax.numpy as jnp
from jax import lax
from jax.experimental import pallas as pl
from jax.experimental.pallas import tpu as pltpu
from jax.sharding import PartitionSpec as P

masked_score = -1e30
start_peak = -5e29
GROUP = 4
LEAD = 4
VMEM = pl.BlockSpec(memory_space=pltpu.VMEM)
SMEM = pl.BlockSpec(memory_space=pltpu.SMEM)
ANY = pl.BlockSpec(memory_space=pl.ANY)
f32, bf16 = jnp.float32, jnp.bfloat16


def limit(mib):
    return pltpu.CompilerParams(vmem_limit_bytes=mib * 2**20)


def in_parts(x):
    first = x.astype(bf16).astype(f32)
    second = (x - first).astype(bf16).astype(f32)
    return first, second, x - first - second


def flatten_heads(values):
    step_count, requests = (values.shape[2], values.shape[0])
    return values.transpose(2, 0, 1, 3, 4).reshape(step_count, requests, -1)


def general(
    cache_keys,
    cache_values,
    slot_req,
    slot_fill,
    mig_src,
    mig_dst,
    queries,
    new_keys,
    new_values,
    out_weight,
):
    slot_count, page_len, kv_local, head_dim = cache_keys.shape
    step_count, requests, heads_local, _ = queries.shape
    group_size = heads_local // kv_local
    score_scale = 1.0 / math.sqrt(head_dim)
    peer_count = lax.axis_size("inst")
    capacity = mig_src.shape[2]
    outgoing = mig_src[0].reshape(-1)
    landing = mig_dst[0].reshape(-1)
    leaving = outgoing >= 0
    picked = jnp.maximum(outgoing, 0)
    parcel = jnp.stack([cache_keys[picked], cache_values[picked]], axis=1)
    parcel = parcel.reshape(peer_count, capacity, 2, page_len, kv_local, head_dim)
    labels = jnp.stack([slot_req[picked], slot_fill[picked], landing], axis=1).reshape(
        peer_count, capacity, 3
    )
    arrived, arrived_labels = (
        lax.all_to_all(parcel, "inst", split_axis=0, concat_axis=0, tiled=True),
        lax.all_to_all(labels, "inst", split_axis=0, concat_axis=0, tiled=True),
    )
    arrived = arrived.reshape(peer_count * capacity, 2, page_len, kv_local, head_dim)
    arrived_labels = arrived_labels.reshape(peer_count * capacity, 3)
    vacated = jnp.where(leaving, outgoing, slot_count)
    target = jnp.where(arrived_labels[:, 2] >= 0, arrived_labels[:, 2], slot_count)
    moved_keys = (
        cache_keys.at[vacated]
        .set(jnp.zeros_like(parcel[0, 0, 0]), mode="drop")
        .at[target]
        .set(arrived[:, 0], mode="drop")
    )
    moved_values = (
        cache_values.at[vacated]
        .set(jnp.zeros_like(parcel[0, 0, 1]), mode="drop")
        .at[target]
        .set(arrived[:, 1], mode="drop")
    )
    moved_req = slot_req.at[target].set(arrived_labels[:, 0], mode="drop")
    moved_fill = (
        slot_fill.at[vacated].set(0, mode="drop").at[target].set(arrived_labels[:, 1], mode="drop")
    )
    keys, values, req_used, fill_used = (moved_keys, moved_values, moved_req, moved_fill)
    grouped = queries.reshape(step_count, requests, kv_local, group_size, head_dim)
    chosen = grouped[:, req_used]
    scores = (
        jnp.einsum("snkgd,ntkd->nksgt", chosen, keys, preferred_element_type=jnp.float32)
        * score_scale
    )
    live_tokens = jnp.arange(page_len, dtype=jnp.int32)[None, :] < fill_used[:, None]
    live_full = live_tokens[:, None, None, None, :]
    scores = jnp.where(live_full, scores, masked_score)
    page_peak = scores.max(-1)
    weights = jnp.where(live_full, jnp.exp(scores - page_peak[..., None]), 0.0)
    weight_sum = weights.sum(-1)
    per_slot = jnp.einsum(
        "nksgt,ntkd->nksgd",
        weights.astype(jnp.bfloat16),
        values,
        preferred_element_type=jnp.float32,
    )
    members = jnp.arange(requests, dtype=jnp.int32)
    onehot = req_used[:, None] == members[None, :]
    indicator = onehot.astype(jnp.float32)
    local_peak = jnp.where(onehot[:, :, None, None, None], page_peak[:, None], masked_score).max(0)
    fresh_part = (
        jnp.einsum("srkgd,urkd->rksgu", grouped, new_keys, preferred_element_type=jnp.float32)
        * score_scale
    )
    causal = jnp.arange(step_count)[None, :] <= jnp.arange(step_count)[:, None]
    fresh_part = jnp.where(causal[None, None, :, None, :], fresh_part, masked_score)
    fresh_peak = fresh_part.max(-1)
    fresh_weights = jnp.exp(fresh_part - fresh_peak[..., None])
    fresh_numerator = jnp.einsum(
        "rksgu,urkd->rksgd",
        fresh_weights.astype(jnp.bfloat16),
        new_values,
        preferred_element_type=jnp.float32,
    )
    fresh_denominator = fresh_weights.sum(-1)
    score_peak = lax.pmax(jnp.maximum(local_peak, fresh_peak), "inst")
    factor = jnp.exp(page_peak - score_peak[req_used])
    numerator = jnp.einsum(
        "nr,nksgd->rksgd", indicator, per_slot * factor[..., None], precision=lax.Precision.HIGHEST
    )
    denominator = jnp.einsum(
        "nr,nksg->rksg", indicator, weight_sum * factor, precision=lax.Precision.HIGHEST
    )
    fresh_factor = jnp.exp(fresh_peak - score_peak)
    numerator, denominator, fresh_numer, fresh_denom = (
        numerator,
        denominator,
        fresh_numerator * fresh_factor[..., None],
        fresh_denominator * fresh_factor,
    )
    share_width = heads_local * head_dim // peer_count
    numerator_share = lax.psum_scatter(
        flatten_heads(numerator), "inst", scatter_dimension=2, tiled=True
    )
    denominator_all = lax.psum(denominator, "inst")
    full_denominator = flatten_heads(
        jnp.broadcast_to((denominator_all + fresh_denom)[..., None], fresh_numer.shape)
    )
    offset_start = lax.axis_index("inst") * share_width
    fresh_share = lax.dynamic_slice_in_dim(flatten_heads(fresh_numer), offset_start, share_width, 2)
    share_part = (numerator_share + fresh_share) / lax.dynamic_slice_in_dim(
        full_denominator, offset_start, share_width, 2
    )
    attention = lax.all_gather(share_part.astype(jnp.bfloat16), "inst", axis=2, tiled=True)
    attention = attention.reshape(step_count * requests, heads_local * head_dim)
    projected = jnp.dot(attention, out_weight, preferred_element_type=jnp.float32).reshape(
        step_count, requests, -1
    )
    output = lax.psum_scatter(projected, "head", scatter_dimension=2, tiled=True).astype(
        jnp.bfloat16
    )
    return (moved_keys, moved_values, output)


def attention_kernel(
    req_ref, fill_ref, q_ref, k_vmem, v_vmem,
    out_ref,
    q_turned, k_wide, v_wide, k_ready, v_ready, scores, fresh_peak, weights, factor_ref,
    peak, total, old_peak, old_total, acc, lse_acc,
    order, order_fill, item_req, count,
):
    slots, rows, head_dim = k_vmem.shape
    steps, requests, heads, _ = q_ref.shape
    kv_local = q_turned.shape[1]
    page = rows // kv_local
    group = heads // kv_local
    q_rows = steps * group
    tokens = GROUP * page
    f32, bf16 = jnp.float32, jnp.bfloat16
    scale = math.log2(math.e) / math.sqrt(head_dim)
    peers, chunk_rows, _ = out_ref.shape
    near = steps // peers
    body_rows = near * requests * heads

    def clear(r, _):
        count[r] = 0
        return 0

    lax.fori_loop(0, requests, clear, 0)

    def tally(i, _):
        r = req_ref[i]
        count[r] = count[r] + (fill_ref[i] > 0).astype(jnp.int32)
        return 0

    lax.fori_loop(0, slots, tally, 0, unroll=8)
    def blank(item, r):
        item_req[item] = r
        for g in range(GROUP):
            order[item * GROUP + g] = 0
            order_fill[item * GROUP + g] = 0
    for item in range(LEAD):
        blank(item, -1)

    def place(r, item):
        items = (count[r] + GROUP - 1) // GROUP
        count[r] = item * GROUP
        last = item + items - 1

        @pl.when(items > 0)
        def _():
            blank(last, r)

        def name(j, _):
            item_req[j] = r
            return 0

        lax.fori_loop(item, last, name, 0)
        return last + 1

    end = lax.fori_loop(0, requests, place, LEAD)
    for item in range(LEAD):
        blank(end + item, -1)

    def insert(i, _):
        fill = fill_ref[i]

        @pl.when(fill > 0)
        def _():
            r = req_ref[i]
            at = count[r]
            order[at] = i
            order_fill[at] = fill
            count[r] = at + 1

        return 0

    lax.fori_loop(0, slots, insert, 0, unroll=8)

    def turn(r, _):
        for k in range(kv_local):
            q_turned[r, k] = q_ref[:, r, k * group : (k + 1) * group, :].reshape(q_rows, head_dim).T
        return 0

    lax.fori_loop(0, requests, turn, 0, unroll=2)
    out_ref[...] = jnp.zeros_like(out_ref)
    lse_acc[...] = jnp.full(lse_acc.shape, masked_score, f32)
    for ref in (acc, weights, scores, peak, total, old_peak, old_total, fresh_peak, factor_ref, k_ready, v_ready):
        ref[...] = jnp.zeros_like(ref)
    token = lax.broadcasted_iota(jnp.int32, (page, q_rows), 0)

    def finish(t):
        r = item_req[t]

        @pl.when((r >= 0) & (item_req[t + 1] != r))
        def _():
            for k in range(kv_local):
                l = old_total[k].sum(axis=0, keepdims=True)
                o = (acc[k] * (1.0 / l)).T
                o = o.astype(bf16)
                for s in range(steps):
                    at = ((s % near) * requests + r) * heads + k * group
                    out_ref[s // near, pl.ds(pl.multiple_of(at, group), group), :] = o[s * group : (s + 1) * group]
                lse_acc[pl.ds(r * kv_local + k, 1), :] = old_peak[k, :1] + jnp.log2(l)

    def collect(t):
        for k in range(kv_local):
            pv = jnp.dot(v_ready[k], weights[k], preferred_element_type=f32)
            acc[k] = acc[k] * factor_ref[k, :1] + pv

    def soften(t):
        first = item_req[t] != item_req[t - 1]
        for k in range(kv_local):
            before = peak[k]
            sums = total[k]
            old_peak[k] = before
            old_total[k] = sums
            before = jnp.where(first, start_peak, before)
            m = jnp.maximum(before, fresh_peak[k])
            factor = jnp.exp2(before - m)
            peak[k] = m
            factor_ref[k] = factor
            parts = []
            add = jnp.zeros((8, q_rows), f32)
            for a in range(0, tokens, 16):
                p = [jnp.exp2(scores[k, b : b + 8] * scale - m) for b in (a, a + 8)]
                add = add + (p[0] + p[1])
                weights[k, a : a + 16] = jnp.concatenate(p, axis=0).astype(bf16)
            total[k] = sums * factor + add

    def score(t):
        r = jnp.maximum(item_req[t], 0)
        for k in range(kv_local):
            s = jnp.dot(k_ready[k], q_turned[r, k], preferred_element_type=f32)
            high = jnp.full((8, q_rows), -3e30, f32)
            for g in range(GROUP):
                part = jnp.where(token < order_fill[t * GROUP + g], s[g * page : (g + 1) * page], masked_score / scale)
                scores[k, g * page : (g + 1) * page] = part
                for a in range(0, page, 8):
                    high = jnp.maximum(high, part[a : a + 8])
            fresh_peak[k] = jnp.broadcast_to(high.max(axis=0, keepdims=True) * scale, (8, q_rows))

    def ready(t, source, wide):
        for g in range(GROUP):
            wide[g * rows : (g + 1) * rows, :] = source[order[t * GROUP + g]].astype(f32)
        for k in range(kv_local):
            part = pl.ds(k, tokens, stride=kv_local) if kv_local > 1 else pl.ds(0, tokens)
            yield k, wide[part, :].astype(bf16)

    def step(t, _):
        finish(t - 4)
        collect(t - 3)
        soften(t - 2)
        score(t - 1)
        for k, keys in ready(t, k_vmem, k_wide):
            k_ready[k] = keys
        for k, values in ready(t - 2, v_vmem, v_wide):
            v_ready[k] = values.T
        return 0

    lax.fori_loop(LEAD, end + LEAD, step, 0)
    first, second, third = in_parts(lse_acc[...].T)
    lane = lax.broadcasted_iota(jnp.int32, (q_rows, head_dim), 1)
    slot = head_dim // 4
    packed = jnp.where(lane < slot, first, pltpu.roll(second, slot, 1))
    packed = jnp.where(lane < 2 * slot, packed, pltpu.roll(third, 2 * slot, 1)).astype(bf16)
    for j in range(peers):
        out_ref[j, body_rows:, :] = packed[j * near * group : (j + 1) * near * group]


def local_attention(keys, values, slot_req, slot_fill, queries, kv_local, peers):
    slots, rows, head_dim = keys.shape
    steps, requests, heads, _ = queries.shape
    q_rows = steps * heads // kv_local
    tokens = GROUP * rows // kv_local
    items = slots // GROUP + requests + 2 * LEAD
    stat = pltpu.VMEM((kv_local, 8, q_rows), f32)
    chunk = steps // peers * (requests * heads + heads // kv_local)
    return pl.pallas_call(
        attention_kernel,
        out_shape=jax.ShapeDtypeStruct((peers, chunk, head_dim), bf16),
        in_specs=[SMEM, SMEM, VMEM, VMEM, VMEM],
        out_specs=VMEM,
        scratch_shapes=[
            pltpu.VMEM((requests, kv_local, head_dim, q_rows), bf16),
            pltpu.VMEM((GROUP * rows, head_dim), f32),
            pltpu.VMEM((GROUP * rows, head_dim), f32),
            pltpu.VMEM((kv_local, tokens, head_dim), bf16),
            pltpu.VMEM((kv_local, head_dim, tokens), bf16),
            pltpu.VMEM((kv_local, tokens, q_rows), f32),
            stat,
            pltpu.VMEM((kv_local, tokens, q_rows), bf16),
            stat, stat, stat, stat, stat,
            pltpu.VMEM((kv_local, head_dim, q_rows), f32),
            pltpu.VMEM((head_dim, q_rows), f32),
            pltpu.SMEM((items * GROUP,), jnp.int32),
            pltpu.SMEM((items * GROUP,), jnp.int32),
            pltpu.SMEM((items,), jnp.int32),
            pltpu.SMEM((requests,), jnp.int32),
        ],
        compiler_params=limit(32),
        cost_estimate=pl.CostEstimate(flops=3 * 10**9, bytes_accessed=2**24, transcendentals=10**7),
    )(slot_req, slot_fill, queries, keys, values)


def pack_kernel(src_ref, dst_ref, k_ref, v_ref, parcel_ref, label, sems):
    peers, length, lanes = parcel_ref.shape
    slots, rows, _ = k_ref.shape
    capacity = src_ref.shape[0] // peers
    copies = []
    for j in range(peers):
        for c in range(capacity):
            n = jnp.maximum(src_ref[j * capacity + c], 0)
            for i, ref in enumerate((k_ref, v_ref)):
                a = i * capacity + c
                copies.append(
                    pltpu.make_async_copy(
                        ref.at[n], parcel_ref.at[j, pl.ds(a * rows, rows)], sems.at[j, a]
                    )
                )
                copies[-1].start()
    lane = lax.broadcasted_iota(jnp.int32, label.shape[1:], 1)
    for j in range(peers):
        word = jnp.zeros(label.shape[1:], jnp.int32)
        for c in range(capacity):
            word = jnp.where(lane == c, dst_ref[j * capacity + c], word)
        label[j] = word.astype(f32).astype(bf16)
    body = 2 * capacity * rows
    last = pltpu.make_async_copy(
        label, parcel_ref.at[:, pl.ds(body, length - body)], sems.at[0, 2 * capacity]
    )
    last.start()
    for copy in copies:
        copy.wait()
    last.wait()


def pack(keys, values, outgoing, landing, peers):
    slots, rows, lanes = keys.shape
    capacity = outgoing.shape[0] // peers
    return pl.pallas_call(
        pack_kernel,
        out_shape=jax.ShapeDtypeStruct((peers, 2 * capacity * rows + 16, lanes), bf16),
        in_specs=[SMEM, SMEM, ANY, ANY],
        out_specs=ANY,
        scratch_shapes=[
            pltpu.VMEM((peers, 16, lanes), bf16),
            pltpu.SemaphoreType.DMA((peers, 2 * capacity + 1)),
        ],
    )(outgoing, landing, keys, values)


def place_kernel(src_ref, target_ref, k_ref, v_ref, arrived_ref, mk_ref, mv_ref, blank, sems, page_sems, zero_sems):
    slots, rows, _ = k_ref.shape
    peers = arrived_ref.shape[0]
    capacity = src_ref.shape[0] // peers
    parts = sems.shape[1]
    per = slots // parts
    copies = []
    for p in range(parts):
        for i, (a, b) in enumerate(((k_ref, mk_ref), (v_ref, mv_ref))):
            part = pl.ds(p * per, per)
            copies.append(pltpu.make_async_copy(a.at[part], b.at[part], sems.at[i, p]))
            copies[-1].start()
    blank[...] = jnp.zeros_like(blank)
    for copy in copies:
        copy.wait()

    def each(act):
        for i, ref in enumerate((mk_ref, mv_ref)):
            for j in range(peers):
                for c in range(capacity):
                    leaving = src_ref[j * capacity + c]
                    taken = target_ref[j * capacity + c]

                    @pl.when(leaving >= 0)
                    def _():
                        act(pltpu.make_async_copy(blank, ref.at[leaving], zero_sems.at[i, j, c]))

                    @pl.when(taken >= 0)
                    def _():
                        part = pl.ds((i * capacity + c) * rows, rows)
                        act(pltpu.make_async_copy(arrived_ref.at[j, part], ref.at[taken], page_sems.at[i, j, c]))

    each(lambda copy: copy.start())
    each(lambda copy: copy.wait())


def place(keys, values, arrived, outgoing, target):
    slots, rows, lanes = keys.shape
    peers = arrived.shape[0]
    capacity = outgoing.shape[0] // peers
    each = pltpu.SemaphoreType.DMA((2, peers, capacity))
    return pl.pallas_call(
        place_kernel,
        out_shape=(jax.ShapeDtypeStruct(keys.shape, bf16),) * 2,
        in_specs=[SMEM, SMEM, ANY, ANY, ANY],
        out_specs=(ANY, ANY),
        scratch_shapes=[
            pltpu.VMEM((rows, lanes), bf16),
            pltpu.SemaphoreType.DMA((2, 8)),
            each,
            each,
        ],
        cost_estimate=pl.CostEstimate(flops=0, bytes_accessed=2**25, transcendentals=0),
    )(outgoing, target, keys, values, arrived)


def fresh_kernel(q_ref, nk_ref, nv_ref, mine_ref, out_ref, lse_ref, *, kv_local):
    near, requests, heads, head_dim = q_ref.shape
    steps = nk_ref.shape[0]
    group = heads // kv_local
    rows = near * group
    scale = math.log2(math.e) / math.sqrt(head_dim)
    step = lax.broadcasted_iota(jnp.int32, (rows, steps), 0) // group + mine_ref[0] * near
    live = lax.broadcasted_iota(jnp.int32, (rows, steps), 1) <= step
    lane = lax.broadcasted_iota(jnp.int32, (rows, head_dim), 1)
    lse = jnp.zeros((rows, head_dim), f32)
    for r in range(requests):
        for k in range(kv_local):
            n = r * kv_local + k
            q = q_ref[:, r, k * group : (k + 1) * group, :].reshape(rows, head_dim)
            s = lax.dot_general(q, nk_ref[:, n, :].astype(bf16), (((1,), (1,)), ((), ())), preferred_element_type=f32)
            s = jnp.where(live, s * scale, masked_score)
            m = s.max(axis=1, keepdims=True)
            p = jnp.exp2(s - m)
            l = p.sum(axis=1, keepdims=True)
            o = jnp.dot(p.astype(bf16), nv_ref[:, n, :].astype(bf16), preferred_element_type=f32) * (1.0 / l)
            out_ref[:, r, k * group : (k + 1) * group, :] = o.reshape(near, group, head_dim)
            lse = jnp.where(lane == n, m + jnp.log2(l), lse)
    lse_ref[...] = lse


def fresh_part(queries, new_keys, new_values, mine, kv_local):
    near, requests, heads, head_dim = queries.shape
    steps = new_keys.shape[0]
    wide = (steps, requests * kv_local, head_dim)
    return pl.pallas_call(
        functools.partial(fresh_kernel, kv_local=kv_local),
        out_shape=(
            jax.ShapeDtypeStruct(queries.shape, f32),
            jax.ShapeDtypeStruct((near * heads // kv_local, head_dim), f32),
        ),
        in_specs=[VMEM, VMEM, VMEM, SMEM],
        out_specs=(VMEM, VMEM),
        compiler_params=limit(16),
        cost_estimate=pl.CostEstimate(flops=10**8, bytes_accessed=2**21, transcendentals=10**5),
    )(queries, new_keys.astype(f32).reshape(wide), new_values.astype(f32).reshape(wide), mine)


def combine_kernel(parts_ref, fresh_ref, fresh_lse_ref, out_ref, rows_ref, *, kv_local):
    peers = parts_ref.shape[0]
    near, requests, heads, head_dim = fresh_ref.shape
    group = heads // kv_local
    body = near * requests * heads
    slot = head_dim // 4
    peaks = [fresh_lse_ref[...]]
    for i in range(peers):
        x = parts_ref[i, body:, :].astype(f32)
        peaks.append(x + pltpu.roll(x, head_dim - slot, 1) + pltpu.roll(x, head_dim - 2 * slot, 1))
    top = functools.reduce(jnp.maximum, peaks)
    shares = [jnp.exp2(x - top) for x in peaks]
    whole = 1.0 / functools.reduce(jnp.add, shares)
    shares = [x * whole for x in shares]
    for r in range(requests):
        for k in range(kv_local):
            n = r * kv_local + k
            cols = [x[:, n : n + 1] for x in shares]
            o = fresh_ref[:, r, k * group : (k + 1) * group, :].reshape(near * group, head_dim) * cols[0]
            for i in range(peers):
                part = [
                    parts_ref[i, pl.ds((s * requests + r) * heads + k * group, group), :].astype(f32)
                    for s in range(near)
                ]
                o = o + jnp.concatenate(part, axis=0) * cols[i + 1]
            for s in range(near):
                rows_ref[pl.ds((s * requests + r) * heads + k * group, group), :] = o[s * group : (s + 1) * group]
    for h in range(heads):
        out_ref[:, h * head_dim : (h + 1) * head_dim] = rows_ref[pl.ds(h, near * requests, stride=heads), :].astype(bf16)


def combine(parts, fresh, fresh_lse, kv_local):
    near, requests, heads, head_dim = fresh.shape
    return pl.pallas_call(
        functools.partial(combine_kernel, kv_local=kv_local),
        out_shape=jax.ShapeDtypeStruct((near * requests, heads * head_dim), bf16),
        in_specs=[VMEM] * 3,
        out_specs=VMEM,
        scratch_shapes=[pltpu.VMEM((near * requests * heads, head_dim), f32)],
        compiler_params=limit(16),
    )(parts, fresh, fresh_lse)


def project_kernel(mine_ref, *refs, sides):
    blocks, (w_ref, out_ref, rows_ref, sums_ref) = refs[:-4], refs[-4:]
    rows = blocks[0].shape[0]
    for i, block in enumerate(blocks):
        rows_ref[i * rows : (i + 1) * rows, :] = block[...].astype(f32)
    width = w_ref.shape[1] // sides
    x = rows_ref[...].astype(bf16)
    for b in range(sides):
        sums_ref[b] = jnp.dot(x, w_ref[:, b * width : (b + 1) * width], preferred_element_type=f32)
    for p in range(sides):
        out_ref[p] = sums_ref[p ^ mine_ref[0]].astype(bf16)


def project(blocks, weight, mine, sides):
    rows, depth = blocks[0].shape
    rows *= len(blocks)
    width = weight.shape[1] // sides
    return pl.pallas_call(
        functools.partial(project_kernel, sides=sides),
        out_shape=jax.ShapeDtypeStruct((sides, rows, width), bf16),
        in_specs=[SMEM] + [VMEM] * (len(blocks) + 1),
        out_specs=VMEM,
        scratch_shapes=[pltpu.VMEM((rows, depth), f32), pltpu.VMEM((sides, rows, width), f32)],
        compiler_params=limit(40),
    )(mine, *blocks, weight)


def mirrored(axis, k):
    return [(i, i ^ k) for i in range(lax.axis_size(axis))]


def gather_over(x, axis):
    count = lax.axis_size(axis)
    got = {0: x}
    for k in range(2, count, 2):
        got[k] = lax.ppermute(x, axis, mirrored(axis, k))
    for k in range(0, count, 2):
        got[k + 1] = lax.ppermute(got[k], axis, mirrored(axis, 1))
    return [got[k] for k in range(count)]


def shards(cache_keys, cache_values, slot_req, slot_fill, mig_src, mig_dst, queries, new_keys, new_values, out_weight):
    slots, page, kv_local, head_dim = cache_keys.shape
    steps, requests, heads, _ = queries.shape
    peers, sides = lax.axis_size("inst"), lax.axis_size("head")
    if steps % peers or sides != 4 or peers & (peers - 1) or slots > 256:
        return general(
            cache_keys, cache_values, slot_req, slot_fill, mig_src, mig_dst, queries, new_keys, new_values, out_weight
        )
    near = steps // peers
    me = lax.axis_index("inst")
    mine = me.reshape(1).astype(jnp.int32)
    side = lax.axis_index("head").reshape(1).astype(jnp.int32)
    rows = page * kv_local
    capacity = mig_src.shape[2]
    keys = cache_keys.reshape(slots, rows, head_dim)
    values = cache_values.reshape(slots, rows, head_dim)
    outgoing, landing = mig_src.reshape(-1), mig_dst.reshape(-1)
    parcel = pack(keys, values, outgoing, landing, peers)
    arrived = lax.all_to_all(parcel, "inst", split_axis=0, concat_axis=0, tiled=True)
    target = arrived[:, 2 * capacity * rows, :capacity].astype(jnp.int32).reshape(-1)
    moved_keys, moved_values = place(keys, values, arrived, outgoing, target)

    parts = local_attention(keys, values, slot_req, slot_fill, queries, kv_local, peers)
    parts = lax.all_to_all(parts, "inst", split_axis=0, concat_axis=0, tiled=True)
    own = lax.dynamic_slice_in_dim(queries, me * near, near, 0)
    fresh, fresh_lse = fresh_part(own, new_keys, new_values, mine, kv_local)
    blocks = gather_over(combine(parts, fresh, fresh_lse, kv_local), "inst")
    shares = project(blocks, out_weight, side, sides)
    lent = lax.ppermute(jnp.stack([shares[1], shares[3]]), "head", mirrored("head", 1))
    kept = shares[0].astype(f32) + lent[0].astype(f32)
    passed = (shares[2].astype(f32) + lent[1].astype(f32)).astype(bf16)
    total = kept + lax.ppermute(passed, "head", mirrored("head", 2)).astype(f32)
    total = total.astype(bf16).reshape(peers, near, requests, -1)
    output = jnp.take(total, jnp.arange(peers) ^ me, axis=0).reshape(steps, requests, -1)
    return moved_keys.reshape(cache_keys.shape), moved_values.reshape(cache_values.shape), output


def solution(mesh):
    in_specs = (
        P("inst", None, "head", None),
        P("inst", None, "head", None),
        P("inst"),
        P("inst"),
        P("inst", None, None),
        P("inst", None, None),
        P(None, None, "head", None),
        P(None, None, "head", None),
        P(None, None, "head", None),
        P("head", "inst"),
    )
    out_specs = (
        P("inst", None, "head", None),
        P("inst", None, "head", None),
        P(None, None, ("inst", "head")),
    )
    return jax.shard_map(shards, mesh=mesh, in_specs=in_specs, out_specs=out_specs, check_vma=False)
```

```python
import functools
import math

import jax
import jax.numpy as jnp
from jax import lax
from jax.experimental import pallas as pl
from jax.experimental.pallas import tpu as pltpu
from jax.sharding import PartitionSpec as P

masked_score = -1e30
start_peak = -5e29
GROUP = 4
LEAD = 4
VMEM = pl.BlockSpec(memory_space=pltpu.VMEM)
SMEM = pl.BlockSpec(memory_space=pltpu.SMEM)
ANY = pl.BlockSpec(memory_space=pl.ANY)
f32, bf16 = jnp.float32, jnp.bfloat16


def limit(mib):
    return pltpu.CompilerParams(vmem_limit_bytes=mib * 2**20)


def in_parts(x):
    first = x.astype(bf16).astype(f32)
    second = (x - first).astype(bf16).astype(f32)
    return first, second, x - first - second


def flatten_heads(values):
    step_count, requests = (values.shape[2], values.shape[0])
    return values.transpose(2, 0, 1, 3, 4).reshape(step_count, requests, -1)


def general(
    cache_keys,
    cache_values,
    slot_req,
    slot_fill,
    mig_src,
    mig_dst,
    queries,
    new_keys,
    new_values,
    out_weight,
):
    slot_count, page_len, kv_local, head_dim = cache_keys.shape
    step_count, requests, heads_local, _ = queries.shape
    group_size = heads_local // kv_local
    score_scale = 1.0 / math.sqrt(head_dim)
    peer_count = lax.axis_size("inst")
    capacity = mig_src.shape[2]
    outgoing = mig_src[0].reshape(-1)
    landing = mig_dst[0].reshape(-1)
    leaving = outgoing >= 0
    picked = jnp.maximum(outgoing, 0)
    parcel = jnp.stack([cache_keys[picked], cache_values[picked]], axis=1)
    parcel = parcel.reshape(peer_count, capacity, 2, page_len, kv_local, head_dim)
    labels = jnp.stack([slot_req[picked], slot_fill[picked], landing], axis=1).reshape(
        peer_count, capacity, 3
    )
    arrived, arrived_labels = (
        lax.all_to_all(parcel, "inst", split_axis=0, concat_axis=0, tiled=True),
        lax.all_to_all(labels, "inst", split_axis=0, concat_axis=0, tiled=True),
    )
    arrived = arrived.reshape(peer_count * capacity, 2, page_len, kv_local, head_dim)
    arrived_labels = arrived_labels.reshape(peer_count * capacity, 3)
    vacated = jnp.where(leaving, outgoing, slot_count)
    target = jnp.where(arrived_labels[:, 2] >= 0, arrived_labels[:, 2], slot_count)
    moved_keys = (
        cache_keys.at[vacated]
        .set(jnp.zeros_like(parcel[0, 0, 0]), mode="drop")
        .at[target]
        .set(arrived[:, 0], mode="drop")
    )
    moved_values = (
        cache_values.at[vacated]
        .set(jnp.zeros_like(parcel[0, 0, 1]), mode="drop")
        .at[target]
        .set(arrived[:, 1], mode="drop")
    )
    moved_req = slot_req.at[target].set(arrived_labels[:, 0], mode="drop")
    moved_fill = (
        slot_fill.at[vacated].set(0, mode="drop").at[target].set(arrived_labels[:, 1], mode="drop")
    )
    keys, values, req_used, fill_used = (moved_keys, moved_values, moved_req, moved_fill)
    grouped = queries.reshape(step_count, requests, kv_local, group_size, head_dim)
    chosen = grouped[:, req_used]
    scores = (
        jnp.einsum("snkgd,ntkd->nksgt", chosen, keys, preferred_element_type=jnp.float32)
        * score_scale
    )
    live_tokens = jnp.arange(page_len, dtype=jnp.int32)[None, :] < fill_used[:, None]
    live_full = live_tokens[:, None, None, None, :]
    scores = jnp.where(live_full, scores, masked_score)
    page_peak = scores.max(-1)
    weights = jnp.where(live_full, jnp.exp(scores - page_peak[..., None]), 0.0)
    weight_sum = weights.sum(-1)
    per_slot = jnp.einsum(
        "nksgt,ntkd->nksgd",
        weights.astype(jnp.bfloat16),
        values,
        preferred_element_type=jnp.float32,
    )
    members = jnp.arange(requests, dtype=jnp.int32)
    onehot = req_used[:, None] == members[None, :]
    indicator = onehot.astype(jnp.float32)
    local_peak = jnp.where(onehot[:, :, None, None, None], page_peak[:, None], masked_score).max(0)
    fresh_part = (
        jnp.einsum("srkgd,urkd->rksgu", grouped, new_keys, preferred_element_type=jnp.float32)
        * score_scale
    )
    causal = jnp.arange(step_count)[None, :] <= jnp.arange(step_count)[:, None]
    fresh_part = jnp.where(causal[None, None, :, None, :], fresh_part, masked_score)
    fresh_peak = fresh_part.max(-1)
    fresh_weights = jnp.exp(fresh_part - fresh_peak[..., None])
    fresh_numerator = jnp.einsum(
        "rksgu,urkd->rksgd",
        fresh_weights.astype(jnp.bfloat16),
        new_values,
        preferred_element_type=jnp.float32,
    )
    fresh_denominator = fresh_weights.sum(-1)
    score_peak = lax.pmax(jnp.maximum(local_peak, fresh_peak), "inst")
    factor = jnp.exp(page_peak - score_peak[req_used])
    numerator = jnp.einsum(
        "nr,nksgd->rksgd", indicator, per_slot * factor[..., None], precision=lax.Precision.HIGHEST
    )
    denominator = jnp.einsum(
        "nr,nksg->rksg", indicator, weight_sum * factor, precision=lax.Precision.HIGHEST
    )
    fresh_factor = jnp.exp(fresh_peak - score_peak)
    numerator, denominator, fresh_numer, fresh_denom = (
        numerator,
        denominator,
        fresh_numerator * fresh_factor[..., None],
        fresh_denominator * fresh_factor,
    )
    share_width = heads_local * head_dim // peer_count
    numerator_share = lax.psum_scatter(
        flatten_heads(numerator), "inst", scatter_dimension=2, tiled=True
    )
    denominator_all = lax.psum(denominator, "inst")
    full_denominator = flatten_heads(
        jnp.broadcast_to((denominator_all + fresh_denom)[..., None], fresh_numer.shape)
    )
    offset_start = lax.axis_index("inst") * share_width
    fresh_share = lax.dynamic_slice_in_dim(flatten_heads(fresh_numer), offset_start, share_width, 2)
    share_part = (numerator_share + fresh_share) / lax.dynamic_slice_in_dim(
        full_denominator, offset_start, share_width, 2
    )
    attention = lax.all_gather(share_part.astype(jnp.bfloat16), "inst", axis=2, tiled=True)
    attention = attention.reshape(step_count * requests, heads_local * head_dim)
    projected = jnp.dot(attention, out_weight, preferred_element_type=jnp.float32).reshape(
        step_count, requests, -1
    )
    output = lax.psum_scatter(projected, "head", scatter_dimension=2, tiled=True).astype(
        jnp.bfloat16
    )
    return (moved_keys, moved_values, output)


def attention_kernel(
    req_ref, fill_ref, q_ref, k_hbm, v_hbm,
    out_ref, mk_hbm, mv_hbm,
    k_vmem, v_vmem, q_turned, k_wide, v_wide, k_ready, v_ready, scores, fresh_peak, weights, factor_ref,
    peak, total, old_peak, old_total, acc, lse_acc,
    order, order_fill, item_req, count, sems,
):
    slots, rows, head_dim = k_vmem.shape
    steps, requests, heads, _ = q_ref.shape
    kv_local = q_turned.shape[1]
    page = rows // kv_local
    group = heads // kv_local
    q_rows = steps * group
    tokens = GROUP * page
    f32, bf16 = jnp.float32, jnp.bfloat16
    scale = math.log2(math.e) / math.sqrt(head_dim)
    loads = [pltpu.make_async_copy(*x) for x in ((k_hbm, k_vmem, sems.at[0]), (v_hbm, v_vmem, sems.at[1]))]
    stores = [pltpu.make_async_copy(*x) for x in ((k_vmem, mk_hbm, sems.at[2]), (v_vmem, mv_hbm, sems.at[3]))]
    for copy in loads:
        copy.start()
    peers, chunk_rows, _ = out_ref.shape
    near = steps // peers
    body_rows = near * requests * heads

    def clear(r, _):
        count[r] = 0
        return 0

    lax.fori_loop(0, requests, clear, 0)

    def tally(i, _):
        r = req_ref[i]
        count[r] = count[r] + (fill_ref[i] > 0).astype(jnp.int32)
        return 0

    lax.fori_loop(0, slots, tally, 0, unroll=8)
    def blank(item, r):
        item_req[item] = r
        for g in range(GROUP):
            order[item * GROUP + g] = 0
            order_fill[item * GROUP + g] = 0
    for item in range(LEAD):
        blank(item, -1)

    def place(r, item):
        items = (count[r] + GROUP - 1) // GROUP
        count[r] = item * GROUP
        last = item + items - 1

        @pl.when(items > 0)
        def _():
            blank(last, r)

        def name(j, _):
            item_req[j] = r
            return 0

        lax.fori_loop(item, last, name, 0)
        return last + 1

    end = lax.fori_loop(0, requests, place, LEAD)
    for item in range(LEAD):
        blank(end + item, -1)

    def insert(i, _):
        fill = fill_ref[i]

        @pl.when(fill > 0)
        def _():
            r = req_ref[i]
            at = count[r]
            order[at] = i
            order_fill[at] = fill
            count[r] = at + 1

        return 0

    lax.fori_loop(0, slots, insert, 0, unroll=8)

    def turn(r, _):
        for k in range(kv_local):
            q_turned[r, k] = q_ref[:, r, k * group : (k + 1) * group, :].reshape(q_rows, head_dim).T
        return 0

    lax.fori_loop(0, requests, turn, 0, unroll=2)
    out_ref[...] = jnp.zeros_like(out_ref)
    lse_acc[...] = jnp.full(lse_acc.shape, masked_score, f32)
    for ref in (acc, weights, scores, peak, total, old_peak, old_total, fresh_peak, factor_ref, k_ready, v_ready):
        ref[...] = jnp.zeros_like(ref)
    token = lax.broadcasted_iota(jnp.int32, (page, q_rows), 0)
    for load, store in zip(loads, stores):
        load.wait()
        store.start()

    def finish(t):
        r = item_req[t]

        @pl.when((r >= 0) & (item_req[t + 1] != r))
        def _():
            for k in range(kv_local):
                l = old_total[k].sum(axis=0, keepdims=True)
                o = (acc[k] * (1.0 / l)).T
                o = o.astype(bf16)
                for s in range(steps):
                    at = ((s % near) * requests + r) * heads + k * group
                    out_ref[s // near, pl.ds(pl.multiple_of(at, group), group), :] = o[s * group : (s + 1) * group]
                lse_acc[pl.ds(r * kv_local + k, 1), :] = old_peak[k, :1] + jnp.log2(l)

    def collect(t):
        for k in range(kv_local):
            pv = jnp.dot(v_ready[k], weights[k], preferred_element_type=f32)
            acc[k] = acc[k] * factor_ref[k, :1] + pv

    def soften(t):
        first = item_req[t] != item_req[t - 1]
        for k in range(kv_local):
            before = peak[k]
            sums = total[k]
            old_peak[k] = before
            old_total[k] = sums
            before = jnp.where(first, start_peak, before)
            m = jnp.maximum(before, fresh_peak[k])
            factor = jnp.exp2(before - m)
            peak[k] = m
            factor_ref[k] = factor
            parts = []
            add = jnp.zeros((8, q_rows), f32)
            for a in range(0, tokens, 16):
                p = [jnp.exp2(scores[k, b : b + 8] * scale - m) for b in (a, a + 8)]
                add = add + (p[0] + p[1])
                weights[k, a : a + 16] = jnp.concatenate(p, axis=0).astype(bf16)
            total[k] = sums * factor + add

    def score(t):
        r = jnp.maximum(item_req[t], 0)
        for k in range(kv_local):
            s = jnp.dot(k_ready[k], q_turned[r, k], preferred_element_type=f32)
            high = jnp.full((8, q_rows), -3e30, f32)
            for g in range(GROUP):
                part = jnp.where(token < order_fill[t * GROUP + g], s[g * page : (g + 1) * page], masked_score / scale)
                scores[k, g * page : (g + 1) * page] = part
                for a in range(0, page, 8):
                    high = jnp.maximum(high, part[a : a + 8])
            fresh_peak[k] = jnp.broadcast_to(high.max(axis=0, keepdims=True) * scale, (8, q_rows))

    def ready(t, source, wide):
        for g in range(GROUP):
            wide[g * rows : (g + 1) * rows, :] = source[order[t * GROUP + g]].astype(f32)
        for k in range(kv_local):
            part = pl.ds(k, tokens, stride=kv_local) if kv_local > 1 else pl.ds(0, tokens)
            yield k, wide[part, :].astype(bf16)

    def step(t, _):
        finish(t - 4)
        collect(t - 3)
        soften(t - 2)
        score(t - 1)
        for k, keys in ready(t, k_vmem, k_wide):
            k_ready[k] = keys
        for k, values in ready(t - 2, v_vmem, v_wide):
            v_ready[k] = values.T
        return 0

    lax.fori_loop(LEAD, end + LEAD, step, 0)
    first, second, third = in_parts(lse_acc[...].T)
    lane = lax.broadcasted_iota(jnp.int32, (q_rows, head_dim), 1)
    slot = head_dim // 4
    packed = jnp.where(lane < slot, first, pltpu.roll(second, slot, 1))
    packed = jnp.where(lane < 2 * slot, packed, pltpu.roll(third, 2 * slot, 1)).astype(bf16)
    for j in range(peers):
        out_ref[j, body_rows:, :] = packed[j * near * group : (j + 1) * near * group]
    for store in stores:
        store.wait()


def local_attention(keys, values, slot_req, slot_fill, queries, kv_local, peers):
    slots, rows, head_dim = keys.shape
    steps, requests, heads, _ = queries.shape
    q_rows = steps * heads // kv_local
    tokens = GROUP * rows // kv_local
    items = slots // GROUP + requests + 2 * LEAD
    stat = pltpu.VMEM((kv_local, 8, q_rows), f32)
    chunk = steps // peers * (requests * heads + heads // kv_local)
    return pl.pallas_call(
        attention_kernel,
        out_shape=(
            jax.ShapeDtypeStruct((peers, chunk, head_dim), bf16),
            jax.ShapeDtypeStruct(keys.shape, bf16),
            jax.ShapeDtypeStruct(keys.shape, bf16),
        ),
        in_specs=[SMEM, SMEM, VMEM, ANY, ANY],
        out_specs=(VMEM, ANY, ANY),
        scratch_shapes=[
            pltpu.VMEM(keys.shape, bf16),
            pltpu.VMEM(keys.shape, bf16),
            pltpu.VMEM((requests, kv_local, head_dim, q_rows), bf16),
            pltpu.VMEM((GROUP * rows, head_dim), f32),
            pltpu.VMEM((GROUP * rows, head_dim), f32),
            pltpu.VMEM((kv_local, tokens, head_dim), bf16),
            pltpu.VMEM((kv_local, head_dim, tokens), bf16),
            pltpu.VMEM((kv_local, tokens, q_rows), f32),
            stat,
            pltpu.VMEM((kv_local, tokens, q_rows), bf16),
            stat, stat, stat, stat, stat,
            pltpu.VMEM((kv_local, head_dim, q_rows), f32),
            pltpu.VMEM((head_dim, q_rows), f32),
            pltpu.SMEM((items * GROUP,), jnp.int32),
            pltpu.SMEM((items * GROUP,), jnp.int32),
            pltpu.SMEM((items,), jnp.int32),
            pltpu.SMEM((requests,), jnp.int32),
            pltpu.SemaphoreType.DMA((4,)),
        ],
        compiler_params=limit(56),
        cost_estimate=pl.CostEstimate(flops=3 * 10**9, bytes_accessed=2**24, transcendentals=10**7),
    )(slot_req, slot_fill, queries, keys, values)


def pack_kernel(src_ref, dst_ref, k_ref, v_ref, parcel_ref, sems):
    peers, length, lanes = parcel_ref.shape
    slots, rows, _ = k_ref.shape
    capacity = src_ref.shape[0] // peers
    copies = []
    for j in range(peers):
        for c in range(capacity):
            n = jnp.maximum(src_ref[j * capacity + c], 0)
            for i, ref in enumerate((k_ref, v_ref)):
                a = i * capacity + c
                copies.append(
                    pltpu.make_async_copy(
                        ref.at[n], parcel_ref.at[j, pl.ds(a * rows, rows)], sems.at[j, a]
                    )
                )
                copies[-1].start()
    tail = (length - 2 * capacity * rows, lanes)
    lane = lax.broadcasted_iota(jnp.int32, tail, 1)
    for j in range(peers):
        word = jnp.zeros(tail, jnp.int32)
        for c in range(capacity):
            word = jnp.where(lane == c, dst_ref[j * capacity + c], word)
        parcel_ref[j, 2 * capacity * rows :, :] = word.astype(f32).astype(bf16)
    for copy in copies:
        copy.wait()


def pack(keys, values, outgoing, landing, peers):
    slots, rows, lanes = keys.shape
    capacity = outgoing.shape[0] // peers
    return pl.pallas_call(
        pack_kernel,
        out_shape=jax.ShapeDtypeStruct((peers, 2 * capacity * rows + 16, lanes), bf16),
        in_specs=[SMEM, SMEM, ANY, ANY],
        out_specs=VMEM,
        scratch_shapes=[pltpu.SemaphoreType.DMA((peers, 2 * capacity))],
        compiler_params=limit(56),
    )(outgoing, landing, keys, values)


def place_kernel(src_ref, target_ref, arrived_ref, k_ref, v_ref, mk_ref, mv_ref, blank, page_sems, zero_sems):
    rows = k_ref.shape[1]
    peers = arrived_ref.shape[0]
    capacity = src_ref.shape[0] // peers
    blank[...] = jnp.zeros_like(blank)

    def each(act):
        for i, ref in enumerate((mk_ref, mv_ref)):
            for j in range(peers):
                for c in range(capacity):
                    leaving = src_ref[j * capacity + c]
                    taken = target_ref[j * capacity + c]

                    @pl.when(leaving >= 0)
                    def _():
                        act(pltpu.make_async_copy(blank, ref.at[leaving], zero_sems.at[i, j, c]))

                    @pl.when(taken >= 0)
                    def _():
                        part = pl.ds((i * capacity + c) * rows, rows)
                        act(pltpu.make_async_copy(arrived_ref.at[j, part], ref.at[taken], page_sems.at[i, j, c]))

    each(lambda copy: copy.start())
    each(lambda copy: copy.wait())


def place(keys, values, arrived, outgoing, target):
    rows, lanes = keys.shape[1:]
    peers = arrived.shape[0]
    each = pltpu.SemaphoreType.DMA((2, peers, outgoing.shape[0] // peers))
    return pl.pallas_call(
        place_kernel,
        out_shape=(jax.ShapeDtypeStruct(keys.shape, bf16),) * 2,
        in_specs=[SMEM, SMEM, VMEM, ANY, ANY],
        out_specs=(ANY, ANY),
        input_output_aliases={3: 0, 4: 1},
        scratch_shapes=[pltpu.VMEM((rows, lanes), bf16), each, each],
        compiler_params=limit(56),
        cost_estimate=pl.CostEstimate(flops=0, bytes_accessed=2**21, transcendentals=0),
    )(outgoing, target, arrived, keys, values)


def fresh_kernel(q_ref, nk_ref, nv_ref, mine_ref, out_ref, lse_ref, *, kv_local):
    near, requests, heads, head_dim = q_ref.shape
    steps = nk_ref.shape[0]
    group = heads // kv_local
    rows = near * group
    scale = math.log2(math.e) / math.sqrt(head_dim)
    step = lax.broadcasted_iota(jnp.int32, (rows, steps), 0) // group + mine_ref[0] * near
    live = lax.broadcasted_iota(jnp.int32, (rows, steps), 1) <= step
    lane = lax.broadcasted_iota(jnp.int32, (rows, head_dim), 1)
    lse = jnp.zeros((rows, head_dim), f32)
    for r in range(requests):
        for k in range(kv_local):
            n = r * kv_local + k
            q = q_ref[:, r, k * group : (k + 1) * group, :].reshape(rows, head_dim)
            s = lax.dot_general(q, nk_ref[:, n, :].astype(bf16), (((1,), (1,)), ((), ())), preferred_element_type=f32)
            s = jnp.where(live, s * scale, masked_score)
            m = s.max(axis=1, keepdims=True)
            p = jnp.exp2(s - m)
            l = p.sum(axis=1, keepdims=True)
            o = jnp.dot(p.astype(bf16), nv_ref[:, n, :].astype(bf16), preferred_element_type=f32) * (1.0 / l)
            out_ref[:, r, k * group : (k + 1) * group, :] = o.reshape(near, group, head_dim)
            lse = jnp.where(lane == n, m + jnp.log2(l), lse)
    lse_ref[...] = lse


def fresh_part(queries, new_keys, new_values, mine, kv_local):
    near, requests, heads, head_dim = queries.shape
    steps = new_keys.shape[0]
    wide = (steps, requests * kv_local, head_dim)
    return pl.pallas_call(
        functools.partial(fresh_kernel, kv_local=kv_local),
        out_shape=(
            jax.ShapeDtypeStruct(queries.shape, f32),
            jax.ShapeDtypeStruct((near * heads // kv_local, head_dim), f32),
        ),
        in_specs=[VMEM, VMEM, VMEM, SMEM],
        out_specs=(VMEM, VMEM),
        compiler_params=limit(16),
        cost_estimate=pl.CostEstimate(flops=10**8, bytes_accessed=2**21, transcendentals=10**5),
    )(queries, new_keys.astype(f32).reshape(wide), new_values.astype(f32).reshape(wide), mine)


def combine_kernel(parts_ref, fresh_ref, fresh_lse_ref, out_ref, rows_ref, *, kv_local):
    peers = parts_ref.shape[0]
    near, requests, heads, head_dim = fresh_ref.shape
    group = heads // kv_local
    body = near * requests * heads
    slot = head_dim // 4
    peaks = [fresh_lse_ref[...]]
    for i in range(peers):
        x = parts_ref[i, body:, :].astype(f32)
        peaks.append(x + pltpu.roll(x, head_dim - slot, 1) + pltpu.roll(x, head_dim - 2 * slot, 1))
    top = functools.reduce(jnp.maximum, peaks)
    shares = [jnp.exp2(x - top) for x in peaks]
    whole = 1.0 / functools.reduce(jnp.add, shares)
    shares = [x * whole for x in shares]
    for r in range(requests):
        for k in range(kv_local):
            n = r * kv_local + k
            cols = [x[:, n : n + 1] for x in shares]
            o = fresh_ref[:, r, k * group : (k + 1) * group, :].reshape(near * group, head_dim) * cols[0]
            for i in range(peers):
                part = [
                    parts_ref[i, pl.ds((s * requests + r) * heads + k * group, group), :].astype(f32)
                    for s in range(near)
                ]
                o = o + jnp.concatenate(part, axis=0) * cols[i + 1]
            for s in range(near):
                rows_ref[pl.ds((s * requests + r) * heads + k * group, group), :] = o[s * group : (s + 1) * group]
    for h in range(heads):
        out_ref[:, h * head_dim : (h + 1) * head_dim] = rows_ref[pl.ds(h, near * requests, stride=heads), :].astype(bf16)


def combine(parts, fresh, fresh_lse, kv_local):
    near, requests, heads, head_dim = fresh.shape
    return pl.pallas_call(
        functools.partial(combine_kernel, kv_local=kv_local),
        out_shape=jax.ShapeDtypeStruct((near * requests, heads * head_dim), bf16),
        in_specs=[VMEM] * 3,
        out_specs=VMEM,
        scratch_shapes=[pltpu.VMEM((near * requests * heads, head_dim), f32)],
        compiler_params=limit(16),
    )(parts, fresh, fresh_lse)


def project_kernel(mine_ref, *refs, sides):
    blocks, (w_ref, out_ref, rows_ref, sums_ref) = refs[:-4], refs[-4:]
    rows = blocks[0].shape[0]
    for i, block in enumerate(blocks):
        rows_ref[i * rows : (i + 1) * rows, :] = block[...].astype(f32)
    width = w_ref.shape[1] // sides
    x = rows_ref[...].astype(bf16)
    for b in range(sides):
        sums_ref[b] = jnp.dot(x, w_ref[:, b * width : (b + 1) * width], preferred_element_type=f32)
    for p in range(sides):
        out_ref[p] = sums_ref[p ^ mine_ref[0]].astype(bf16)


def project(blocks, weight, mine, sides):
    rows, depth = blocks[0].shape
    rows *= len(blocks)
    width = weight.shape[1] // sides
    return pl.pallas_call(
        functools.partial(project_kernel, sides=sides),
        out_shape=jax.ShapeDtypeStruct((sides, rows, width), bf16),
        in_specs=[SMEM] + [VMEM] * (len(blocks) + 1),
        out_specs=VMEM,
        scratch_shapes=[pltpu.VMEM((rows, depth), f32), pltpu.VMEM((sides, rows, width), f32)],
        compiler_params=limit(40),
    )(mine, *blocks, weight)


def mirrored(axis, k):
    return [(i, i ^ k) for i in range(lax.axis_size(axis))]


def gather_over(x, axis):
    count = lax.axis_size(axis)
    got = {0: x}
    for k in range(2, count, 2):
        got[k] = lax.ppermute(x, axis, mirrored(axis, k))
    for k in range(0, count, 2):
        got[k + 1] = lax.ppermute(got[k], axis, mirrored(axis, 1))
    return [got[k] for k in range(count)]


def shards(cache_keys, cache_values, slot_req, slot_fill, mig_src, mig_dst, queries, new_keys, new_values, out_weight):
    slots, page, kv_local, head_dim = cache_keys.shape
    steps, requests, heads, _ = queries.shape
    peers, sides = lax.axis_size("inst"), lax.axis_size("head")
    if steps % peers or sides != 4 or peers & (peers - 1) or slots > 256:
        return general(
            cache_keys, cache_values, slot_req, slot_fill, mig_src, mig_dst, queries, new_keys, new_values, out_weight
        )
    near = steps // peers
    me = lax.axis_index("inst")
    mine = me.reshape(1).astype(jnp.int32)
    side = lax.axis_index("head").reshape(1).astype(jnp.int32)
    rows = page * kv_local
    capacity = mig_src.shape[2]
    keys = cache_keys.reshape(slots, rows, head_dim)
    values = cache_values.reshape(slots, rows, head_dim)
    outgoing, landing = mig_src.reshape(-1), mig_dst.reshape(-1)
    parcel = pack(keys, values, outgoing, landing, peers)
    parcel, slot_req = lax.optimization_barrier((parcel, slot_req))
    parts, copied_keys, copied_values = local_attention(keys, values, slot_req, slot_fill, queries, kv_local, peers)
    parts = lax.all_to_all(parts, "inst", split_axis=0, concat_axis=0, tiled=True)
    own = lax.dynamic_slice_in_dim(queries, me * near, near, 0)
    fresh, fresh_lse = fresh_part(own, new_keys, new_values, mine, kv_local)
    blocks = gather_over(combine(parts, fresh, fresh_lse, kv_local), "inst")
    parcel, _ = lax.optimization_barrier((parcel, blocks[2::2]))
    arrived = lax.all_to_all(parcel, "inst", split_axis=0, concat_axis=0, tiled=True)
    target = arrived[:, 2 * capacity * rows, :capacity].astype(jnp.int32).reshape(-1)
    moved_keys, moved_values = place(copied_keys, copied_values, arrived, outgoing, target)
    shares = project(blocks, out_weight, side, sides)
    lent = lax.ppermute(jnp.stack([shares[1], shares[3]]), "head", mirrored("head", 1))
    kept = shares[0].astype(f32) + lent[0].astype(f32)
    passed = (shares[2].astype(f32) + lent[1].astype(f32)).astype(bf16)
    total = kept + lax.ppermute(passed, "head", mirrored("head", 2)).astype(f32)
    total = total.astype(bf16).reshape(peers, near, requests, -1)
    output = jnp.take(total, jnp.arange(peers) ^ me, axis=0).reshape(steps, requests, -1)
    return moved_keys.reshape(cache_keys.shape), moved_values.reshape(cache_values.shape), output


def solution(mesh):
    in_specs = (
        P("inst", None, "head", None),
        P("inst", None, "head", None),
        P("inst"),
        P("inst"),
        P("inst", None, None),
        P("inst", None, None),
        P(None, None, "head", None),
        P(None, None, "head", None),
        P(None, None, "head", None),
        P("head", "inst"),
    )
    out_specs = (
        P("inst", None, "head", None),
        P("inst", None, "head", None),
        P(None, None, ("inst", "head")),
    )
    return jax.shard_map(shards, mesh=mesh, in_specs=in_specs, out_specs=out_specs, check_vma=False)
```

```python
import functools
import math

import jax
import jax.numpy as jnp
from jax import lax
from jax.experimental import pallas as pl
from jax.experimental.pallas import tpu as pltpu
from jax.sharding import PartitionSpec as P

masked_score = -1e30
start_peak = -5e29
GROUP = 4
LEAD = 4
VMEM = pl.BlockSpec(memory_space=pltpu.VMEM)
SMEM = pl.BlockSpec(memory_space=pltpu.SMEM)
ANY = pl.BlockSpec(memory_space=pl.ANY)
f32, bf16 = jnp.float32, jnp.bfloat16


def limit(mib):
    return pltpu.CompilerParams(vmem_limit_bytes=mib * 2**20)


def in_parts(x):
    first = x.astype(bf16).astype(f32)
    second = (x - first).astype(bf16).astype(f32)
    return first, second, x - first - second


def flatten_heads(values):
    step_count, requests = (values.shape[2], values.shape[0])
    return values.transpose(2, 0, 1, 3, 4).reshape(step_count, requests, -1)


def general(
    cache_keys,
    cache_values,
    slot_req,
    slot_fill,
    mig_src,
    mig_dst,
    queries,
    new_keys,
    new_values,
    out_weight,
):
    slot_count, page_len, kv_local, head_dim = cache_keys.shape
    step_count, requests, heads_local, _ = queries.shape
    group_size = heads_local // kv_local
    score_scale = 1.0 / math.sqrt(head_dim)
    peer_count = lax.axis_size("inst")
    capacity = mig_src.shape[2]
    outgoing = mig_src[0].reshape(-1)
    landing = mig_dst[0].reshape(-1)
    leaving = outgoing >= 0
    picked = jnp.maximum(outgoing, 0)
    parcel = jnp.stack([cache_keys[picked], cache_values[picked]], axis=1)
    parcel = parcel.reshape(peer_count, capacity, 2, page_len, kv_local, head_dim)
    labels = jnp.stack([slot_req[picked], slot_fill[picked], landing], axis=1).reshape(
        peer_count, capacity, 3
    )
    arrived, arrived_labels = (
        lax.all_to_all(parcel, "inst", split_axis=0, concat_axis=0, tiled=True),
        lax.all_to_all(labels, "inst", split_axis=0, concat_axis=0, tiled=True),
    )
    arrived = arrived.reshape(peer_count * capacity, 2, page_len, kv_local, head_dim)
    arrived_labels = arrived_labels.reshape(peer_count * capacity, 3)
    vacated = jnp.where(leaving, outgoing, slot_count)
    target = jnp.where(arrived_labels[:, 2] >= 0, arrived_labels[:, 2], slot_count)
    moved_keys = (
        cache_keys.at[vacated]
        .set(jnp.zeros_like(parcel[0, 0, 0]), mode="drop")
        .at[target]
        .set(arrived[:, 0], mode="drop")
    )
    moved_values = (
        cache_values.at[vacated]
        .set(jnp.zeros_like(parcel[0, 0, 1]), mode="drop")
        .at[target]
        .set(arrived[:, 1], mode="drop")
    )
    moved_req = slot_req.at[target].set(arrived_labels[:, 0], mode="drop")
    moved_fill = (
        slot_fill.at[vacated].set(0, mode="drop").at[target].set(arrived_labels[:, 1], mode="drop")
    )
    keys, values, req_used, fill_used = (moved_keys, moved_values, moved_req, moved_fill)
    grouped = queries.reshape(step_count, requests, kv_local, group_size, head_dim)
    chosen = grouped[:, req_used]
    scores = (
        jnp.einsum("snkgd,ntkd->nksgt", chosen, keys, preferred_element_type=jnp.float32)
        * score_scale
    )
    live_tokens = jnp.arange(page_len, dtype=jnp.int32)[None, :] < fill_used[:, None]
    live_full = live_tokens[:, None, None, None, :]
    scores = jnp.where(live_full, scores, masked_score)
    page_peak = scores.max(-1)
    weights = jnp.where(live_full, jnp.exp(scores - page_peak[..., None]), 0.0)
    weight_sum = weights.sum(-1)
    per_slot = jnp.einsum(
        "nksgt,ntkd->nksgd",
        weights.astype(jnp.bfloat16),
        values,
        preferred_element_type=jnp.float32,
    )
    members = jnp.arange(requests, dtype=jnp.int32)
    onehot = req_used[:, None] == members[None, :]
    indicator = onehot.astype(jnp.float32)
    local_peak = jnp.where(onehot[:, :, None, None, None], page_peak[:, None], masked_score).max(0)
    fresh_part = (
        jnp.einsum("srkgd,urkd->rksgu", grouped, new_keys, preferred_element_type=jnp.float32)
        * score_scale
    )
    causal = jnp.arange(step_count)[None, :] <= jnp.arange(step_count)[:, None]
    fresh_part = jnp.where(causal[None, None, :, None, :], fresh_part, masked_score)
    fresh_peak = fresh_part.max(-1)
    fresh_weights = jnp.exp(fresh_part - fresh_peak[..., None])
    fresh_numerator = jnp.einsum(
        "rksgu,urkd->rksgd",
        fresh_weights.astype(jnp.bfloat16),
        new_values,
        preferred_element_type=jnp.float32,
    )
    fresh_denominator = fresh_weights.sum(-1)
    score_peak = lax.pmax(jnp.maximum(local_peak, fresh_peak), "inst")
    factor = jnp.exp(page_peak - score_peak[req_used])
    numerator = jnp.einsum(
        "nr,nksgd->rksgd", indicator, per_slot * factor[..., None], precision=lax.Precision.HIGHEST
    )
    denominator = jnp.einsum(
        "nr,nksg->rksg", indicator, weight_sum * factor, precision=lax.Precision.HIGHEST
    )
    fresh_factor = jnp.exp(fresh_peak - score_peak)
    numerator, denominator, fresh_numer, fresh_denom = (
        numerator,
        denominator,
        fresh_numerator * fresh_factor[..., None],
        fresh_denominator * fresh_factor,
    )
    share_width = heads_local * head_dim // peer_count
    numerator_share = lax.psum_scatter(
        flatten_heads(numerator), "inst", scatter_dimension=2, tiled=True
    )
    denominator_all = lax.psum(denominator, "inst")
    full_denominator = flatten_heads(
        jnp.broadcast_to((denominator_all + fresh_denom)[..., None], fresh_numer.shape)
    )
    offset_start = lax.axis_index("inst") * share_width
    fresh_share = lax.dynamic_slice_in_dim(flatten_heads(fresh_numer), offset_start, share_width, 2)
    share_part = (numerator_share + fresh_share) / lax.dynamic_slice_in_dim(
        full_denominator, offset_start, share_width, 2
    )
    attention = lax.all_gather(share_part.astype(jnp.bfloat16), "inst", axis=2, tiled=True)
    attention = attention.reshape(step_count * requests, heads_local * head_dim)
    projected = jnp.dot(attention, out_weight, preferred_element_type=jnp.float32).reshape(
        step_count, requests, -1
    )
    output = lax.psum_scatter(projected, "head", scatter_dimension=2, tiled=True).astype(
        jnp.bfloat16
    )
    return (moved_keys, moved_values, output)


def attention_kernel(
    req_ref, fill_ref, q_ref, k_hbm, v_hbm,
    out_ref, mk_hbm, mv_hbm,
    k_vmem, v_vmem, q_turned, k_wide, v_wide, k_ready, v_ready, scores, fresh_peak, weights, factor_ref,
    peak, total, old_peak, old_total, acc, lse_acc,
    order, order_fill, item_req, count, sems,
):
    slots, rows, head_dim = k_vmem.shape
    steps, requests, heads, _ = q_ref.shape
    kv_local = q_turned.shape[1]
    page = rows // kv_local
    group = heads // kv_local
    q_rows = steps * group
    tokens = GROUP * page
    f32, bf16 = jnp.float32, jnp.bfloat16
    scale = math.log2(math.e) / math.sqrt(head_dim)
    loads = [pltpu.make_async_copy(*x) for x in ((k_hbm, k_vmem, sems.at[0]), (v_hbm, v_vmem, sems.at[1]))]
    stores = [pltpu.make_async_copy(*x) for x in ((k_vmem, mk_hbm, sems.at[2]), (v_vmem, mv_hbm, sems.at[3]))]
    for copy in loads:
        copy.start()
    peers, chunk_rows, _ = out_ref.shape
    near = steps // peers
    body_rows = near * requests * heads

    def clear(r, _):
        count[r] = 0
        return 0

    lax.fori_loop(0, requests, clear, 0)

    def tally(i, _):
        r = req_ref[i]
        count[r] = count[r] + (fill_ref[i] > 0).astype(jnp.int32)
        return 0

    lax.fori_loop(0, slots, tally, 0, unroll=8)
    def blank(item, r):
        item_req[item] = r
        for g in range(GROUP):
            order[item * GROUP + g] = 0
            order_fill[item * GROUP + g] = 0
    for item in range(LEAD):
        blank(item, -1)

    def place(r, item):
        items = (count[r] + GROUP - 1) // GROUP
        count[r] = item * GROUP
        last = item + items - 1

        @pl.when(items > 0)
        def _():
            blank(last, r)

        def name(j, _):
            item_req[j] = r
            return 0

        lax.fori_loop(item, last, name, 0)
        return last + 1

    end = lax.fori_loop(0, requests, place, LEAD)
    for item in range(LEAD):
        blank(end + item, -1)

    def insert(i, _):
        fill = fill_ref[i]

        @pl.when(fill > 0)
        def _():
            r = req_ref[i]
            at = count[r]
            order[at] = i
            order_fill[at] = fill
            count[r] = at + 1

        return 0

    lax.fori_loop(0, slots, insert, 0, unroll=8)

    def turn(r, _):
        for k in range(kv_local):
            q_turned[r, k] = q_ref[:, r, k * group : (k + 1) * group, :].reshape(q_rows, head_dim).T
        return 0

    lax.fori_loop(0, requests, turn, 0, unroll=2)
    out_ref[...] = jnp.zeros_like(out_ref)
    lse_acc[...] = jnp.full(lse_acc.shape, masked_score, f32)
    for ref in (acc, weights, scores, peak, total, old_peak, old_total, fresh_peak, factor_ref, k_ready, v_ready):
        ref[...] = jnp.zeros_like(ref)
    token = lax.broadcasted_iota(jnp.int32, (page, q_rows), 0)
    for load, store in zip(loads, stores):
        load.wait()
        store.start()

    def finish(t):
        r = item_req[t]

        @pl.when((r >= 0) & (item_req[t + 1] != r))
        def _():
            for k in range(kv_local):
                l = old_total[k].sum(axis=0, keepdims=True)
                o = (acc[k] * (1.0 / l)).T
                o = o.astype(bf16)
                for s in range(steps):
                    at = ((s % near) * requests + r) * heads + k * group
                    out_ref[s // near, pl.ds(pl.multiple_of(at, group), group), :] = o[s * group : (s + 1) * group]
                lse_acc[pl.ds(r * kv_local + k, 1), :] = old_peak[k, :1] + jnp.log2(l)

    def collect(t):
        for k in range(kv_local):
            pv = jnp.dot(v_ready[k], weights[k], preferred_element_type=f32)
            acc[k] = acc[k] * factor_ref[k, :1] + pv

    def soften(t):
        first = item_req[t] != item_req[t - 1]
        for k in range(kv_local):
            before = peak[k]
            sums = total[k]
            old_peak[k] = before
            old_total[k] = sums
            before = jnp.where(first, start_peak, before)
            m = jnp.maximum(before, fresh_peak[k])
            factor = jnp.exp2(before - m)
            peak[k] = m
            factor_ref[k] = factor
            parts = []
            add = jnp.zeros((8, q_rows), f32)
            for a in range(0, tokens, 16):
                p = [jnp.exp2(scores[k, b : b + 8] * scale - m) for b in (a, a + 8)]
                add = add + (p[0] + p[1])
                weights[k, a : a + 16] = jnp.concatenate(p, axis=0).astype(bf16)
            total[k] = sums * factor + add

    def score(t):
        r = jnp.maximum(item_req[t], 0)
        for k in range(kv_local):
            s = jnp.dot(k_ready[k], q_turned[r, k], preferred_element_type=f32)
            high = jnp.full((8, q_rows), -3e30, f32)
            for g in range(GROUP):
                part = jnp.where(token < order_fill[t * GROUP + g], s[g * page : (g + 1) * page], masked_score / scale)
                scores[k, g * page : (g + 1) * page] = part
                for a in range(0, page, 8):
                    high = jnp.maximum(high, part[a : a + 8])
            fresh_peak[k] = jnp.broadcast_to(high.max(axis=0, keepdims=True) * scale, (8, q_rows))

    def ready(t, source, wide):
        for g in range(GROUP):
            wide[g * rows : (g + 1) * rows, :] = source[order[t * GROUP + g]].astype(f32)
        for k in range(kv_local):
            part = pl.ds(k, tokens, stride=kv_local) if kv_local > 1 else pl.ds(0, tokens)
            yield k, wide[part, :].astype(bf16)

    def step(t, _):
        finish(t - 4)
        collect(t - 3)
        soften(t - 2)
        score(t - 1)
        for k, keys in ready(t, k_vmem, k_wide):
            k_ready[k] = keys
        for k, values in ready(t - 2, v_vmem, v_wide):
            v_ready[k] = values.T
        return 0

    lax.fori_loop(LEAD, end + LEAD, step, 0)
    first, second, third = in_parts(lse_acc[...].T)
    lane = lax.broadcasted_iota(jnp.int32, (q_rows, head_dim), 1)
    slot = head_dim // 4
    packed = jnp.where(lane < slot, first, pltpu.roll(second, slot, 1))
    packed = jnp.where(lane < 2 * slot, packed, pltpu.roll(third, 2 * slot, 1)).astype(bf16)
    for j in range(peers):
        out_ref[j, body_rows:, :] = packed[j * near * group : (j + 1) * near * group]
    for store in stores:
        store.wait()


def local_attention(keys, values, slot_req, slot_fill, queries, kv_local, peers):
    slots, rows, head_dim = keys.shape
    steps, requests, heads, _ = queries.shape
    q_rows = steps * heads // kv_local
    tokens = GROUP * rows // kv_local
    items = slots // GROUP + requests + 2 * LEAD
    stat = pltpu.VMEM((kv_local, 8, q_rows), f32)
    chunk = steps // peers * (requests * heads + heads // kv_local)
    return pl.pallas_call(
        attention_kernel,
        out_shape=(
            jax.ShapeDtypeStruct((peers, chunk, head_dim), bf16),
            jax.ShapeDtypeStruct(keys.shape, bf16),
            jax.ShapeDtypeStruct(keys.shape, bf16),
        ),
        in_specs=[SMEM, SMEM, VMEM, ANY, ANY],
        out_specs=(VMEM, ANY, ANY),
        scratch_shapes=[
            pltpu.VMEM(keys.shape, bf16),
            pltpu.VMEM(keys.shape, bf16),
            pltpu.VMEM((requests, kv_local, head_dim, q_rows), bf16),
            pltpu.VMEM((GROUP * rows, head_dim), f32),
            pltpu.VMEM((GROUP * rows, head_dim), f32),
            pltpu.VMEM((kv_local, tokens, head_dim), bf16),
            pltpu.VMEM((kv_local, head_dim, tokens), bf16),
            pltpu.VMEM((kv_local, tokens, q_rows), f32),
            stat,
            pltpu.VMEM((kv_local, tokens, q_rows), bf16),
            stat, stat, stat, stat, stat,
            pltpu.VMEM((kv_local, head_dim, q_rows), f32),
            pltpu.VMEM((head_dim, q_rows), f32),
            pltpu.SMEM((items * GROUP,), jnp.int32),
            pltpu.SMEM((items * GROUP,), jnp.int32),
            pltpu.SMEM((items,), jnp.int32),
            pltpu.SMEM((requests,), jnp.int32),
            pltpu.SemaphoreType.DMA((4,)),
        ],
        compiler_params=limit(56),
        cost_estimate=pl.CostEstimate(flops=3 * 10**9, bytes_accessed=2**24, transcendentals=10**7),
    )(slot_req, slot_fill, queries, keys, values)


def pack_kernel(src_ref, dst_ref, k_ref, v_ref, parcel_ref, sems):
    peers, length, lanes = parcel_ref.shape
    slots, rows, _ = k_ref.shape
    capacity = src_ref.shape[0] // peers
    copies = []
    for j in range(peers):
        for c in range(capacity):
            n = jnp.maximum(src_ref[j * capacity + c], 0)
            for i, ref in enumerate((k_ref, v_ref)):
                a = i * capacity + c
                copies.append(
                    pltpu.make_async_copy(
                        ref.at[n], parcel_ref.at[j, pl.ds(a * rows, rows)], sems.at[j, a]
                    )
                )
                copies[-1].start()
    tail = (length - 2 * capacity * rows, lanes)
    lane = lax.broadcasted_iota(jnp.int32, tail, 1)
    for j in range(peers):
        word = jnp.zeros(tail, jnp.int32)
        for c in range(capacity):
            word = jnp.where(lane == c, dst_ref[j * capacity + c], word)
        parcel_ref[j, 2 * capacity * rows :, :] = word.astype(f32).astype(bf16)
    for copy in copies:
        copy.wait()


def pack(keys, values, outgoing, landing, peers):
    slots, rows, lanes = keys.shape
    capacity = outgoing.shape[0] // peers
    return pl.pallas_call(
        pack_kernel,
        out_shape=jax.ShapeDtypeStruct((peers, 2 * capacity * rows + 16, lanes), bf16),
        in_specs=[SMEM, SMEM, ANY, ANY],
        out_specs=VMEM,
        scratch_shapes=[pltpu.SemaphoreType.DMA((peers, 2 * capacity))],
        compiler_params=limit(56),
    )(outgoing, landing, keys, values)


def place_kernel(src_ref, target_ref, arrived_ref, k_ref, v_ref, mk_ref, mv_ref, blank, page_sems, zero_sems):
    rows = k_ref.shape[1]
    peers = arrived_ref.shape[0]
    capacity = src_ref.shape[0] // peers
    blank[...] = jnp.zeros_like(blank)

    def each(act):
        for i, ref in enumerate((mk_ref, mv_ref)):
            for j in range(peers):
                for c in range(capacity):
                    leaving = src_ref[j * capacity + c]
                    taken = target_ref[j * capacity + c]

                    @pl.when(leaving >= 0)
                    def _():
                        act(pltpu.make_async_copy(blank, ref.at[leaving], zero_sems.at[i, j, c]))

                    @pl.when(taken >= 0)
                    def _():
                        part = pl.ds((i * capacity + c) * rows, rows)
                        act(pltpu.make_async_copy(arrived_ref.at[j, part], ref.at[taken], page_sems.at[i, j, c]))

    each(lambda copy: copy.start())
    each(lambda copy: copy.wait())


def place(keys, values, arrived, outgoing, target):
    rows, lanes = keys.shape[1:]
    peers = arrived.shape[0]
    each = pltpu.SemaphoreType.DMA((2, peers, outgoing.shape[0] // peers))
    return pl.pallas_call(
        place_kernel,
        out_shape=(jax.ShapeDtypeStruct(keys.shape, bf16),) * 2,
        in_specs=[SMEM, SMEM, VMEM, ANY, ANY],
        out_specs=(ANY, ANY),
        input_output_aliases={3: 0, 4: 1},
        scratch_shapes=[pltpu.VMEM((rows, lanes), bf16), each, each],
        compiler_params=limit(56),
        cost_estimate=pl.CostEstimate(flops=0, bytes_accessed=2**21, transcendentals=0),
    )(outgoing, target, arrived, keys, values)


def fresh_kernel(q_ref, nk_ref, nv_ref, mine_ref, out_ref, lse_ref, nk_wide, nv_wide, *, kv_local):
    nk_wide[...] = nk_ref[...].astype(f32)
    nv_wide[...] = nv_ref[...].astype(f32)
    near, requests, heads, head_dim = q_ref.shape
    steps = nk_ref.shape[0]
    group = heads // kv_local
    rows = near * group
    scale = math.log2(math.e) / math.sqrt(head_dim)
    step = lax.broadcasted_iota(jnp.int32, (rows, steps), 0) // group + mine_ref[0] * near
    live = lax.broadcasted_iota(jnp.int32, (rows, steps), 1) <= step
    lane = lax.broadcasted_iota(jnp.int32, (rows, head_dim), 1)
    lse = jnp.zeros((rows, head_dim), f32)
    for r in range(requests):
        for k in range(kv_local):
            n = r * kv_local + k
            q = q_ref[:, r, k * group : (k + 1) * group, :].reshape(rows, head_dim)
            s = lax.dot_general(q, nk_wide[:, n, :].astype(bf16), (((1,), (1,)), ((), ())), preferred_element_type=f32)
            s = jnp.where(live, s * scale, masked_score)
            m = s.max(axis=1, keepdims=True)
            p = jnp.exp2(s - m)
            l = p.sum(axis=1, keepdims=True)
            o = jnp.dot(p.astype(bf16), nv_wide[:, n, :].astype(bf16), preferred_element_type=f32) * (1.0 / l)
            out_ref[:, r, k * group : (k + 1) * group, :] = o.reshape(near, group, head_dim)
            lse = jnp.where(lane == n, m + jnp.log2(l), lse)
    lse_ref[...] = lse


def fresh_part(queries, new_keys, new_values, mine, kv_local):
    near, requests, heads, head_dim = queries.shape
    steps = new_keys.shape[0]
    wide = (steps, requests * kv_local, head_dim)
    return pl.pallas_call(
        functools.partial(fresh_kernel, kv_local=kv_local),
        out_shape=(
            jax.ShapeDtypeStruct(queries.shape, f32),
            jax.ShapeDtypeStruct((near * heads // kv_local, head_dim), f32),
        ),
        in_specs=[VMEM, VMEM, VMEM, SMEM],
        out_specs=(VMEM, VMEM),
        scratch_shapes=[pltpu.VMEM(wide, f32)] * 2,
        compiler_params=limit(16),
        cost_estimate=pl.CostEstimate(flops=10**8, bytes_accessed=2**21, transcendentals=10**5),
    )(queries, new_keys.reshape(wide), new_values.reshape(wide), mine)


def combine_kernel(parts_ref, fresh_ref, fresh_lse_ref, out_ref, rows_ref, *, kv_local):
    peers = parts_ref.shape[0]
    near, requests, heads, head_dim = fresh_ref.shape
    group = heads // kv_local
    body = near * requests * heads
    slot = head_dim // 4
    peaks = [fresh_lse_ref[...]]
    for i in range(peers):
        x = parts_ref[i, body:, :].astype(f32)
        peaks.append(x + pltpu.roll(x, head_dim - slot, 1) + pltpu.roll(x, head_dim - 2 * slot, 1))
    top = functools.reduce(jnp.maximum, peaks)
    shares = [jnp.exp2(x - top) for x in peaks]
    whole = 1.0 / functools.reduce(jnp.add, shares)
    shares = [x * whole for x in shares]
    for r in range(requests):
        for k in range(kv_local):
            n = r * kv_local + k
            cols = [x[:, n : n + 1] for x in shares]
            o = fresh_ref[:, r, k * group : (k + 1) * group, :].reshape(near * group, head_dim) * cols[0]
            for i in range(peers):
                part = [
                    parts_ref[i, pl.ds((s * requests + r) * heads + k * group, group), :].astype(f32)
                    for s in range(near)
                ]
                o = o + jnp.concatenate(part, axis=0) * cols[i + 1]
            for s in range(near):
                rows_ref[pl.ds((s * requests + r) * heads + k * group, group), :] = o[s * group : (s + 1) * group]
    for h in range(heads):
        out_ref[:, h * head_dim : (h + 1) * head_dim] = rows_ref[pl.ds(h, near * requests, stride=heads), :].astype(bf16)


def combine(parts, fresh, fresh_lse, kv_local):
    near, requests, heads, head_dim = fresh.shape
    return pl.pallas_call(
        functools.partial(combine_kernel, kv_local=kv_local),
        out_shape=jax.ShapeDtypeStruct((near * requests, heads * head_dim), bf16),
        in_specs=[VMEM] * 3,
        out_specs=VMEM,
        scratch_shapes=[pltpu.VMEM((near * requests * heads, head_dim), f32)],
        compiler_params=limit(16),
    )(parts, fresh, fresh_lse)


def project_kernel(mine_ref, w_ref, *refs, sides):
    blocks, (out_ref, rows_ref, x_ref, panels, sums_ref, sems) = refs[:-6], refs[-6:]
    parts = sems.shape[0]
    deep = w_ref.shape[0] // parts
    copies = [pltpu.make_async_copy(w_ref.at[pl.ds(a * deep, deep)], panels.at[a], sems.at[a]) for a in range(parts)]
    for copy in copies:
        copy.start()
    rows = blocks[0].shape[0]
    for i, block in enumerate(blocks):
        rows_ref[i * rows : (i + 1) * rows, :] = block[...].astype(f32)
    x_ref[...] = rows_ref[...].astype(bf16)
    width = w_ref.shape[1] // sides
    for a, copy in enumerate(copies):
        copy.wait()
        x = x_ref[:, a * deep : (a + 1) * deep]
        for b in range(sides):
            y = jnp.dot(x, panels[a, :, b * width : (b + 1) * width], preferred_element_type=f32)
            sums_ref[b] = y if a == 0 else sums_ref[b] + y
    for p in range(sides):
        out_ref[p] = sums_ref[p ^ mine_ref[0]].astype(bf16)


def project(blocks, weight, mine, sides):
    rows, depth = blocks[0].shape
    rows *= len(blocks)
    width = weight.shape[1] // sides
    parts = 8
    return pl.pallas_call(
        functools.partial(project_kernel, sides=sides),
        out_shape=jax.ShapeDtypeStruct((sides, rows, width), bf16),
        in_specs=[SMEM, ANY] + [VMEM] * len(blocks),
        out_specs=VMEM,
        scratch_shapes=[
            pltpu.VMEM((rows, depth), f32),
            pltpu.VMEM((rows, depth), bf16),
            pltpu.VMEM((parts, depth // parts, weight.shape[1]), bf16),
            pltpu.VMEM((sides, rows, width), f32),
            pltpu.SemaphoreType.DMA((parts,)),
        ],
        compiler_params=limit(54),
    )(mine, weight, *blocks)


def mirrored(axis, k):
    return [(i, i ^ k) for i in range(lax.axis_size(axis))]


def gather_over(x, axis):
    count = lax.axis_size(axis)
    got = {0: x}
    for k in range(2, count, 2):
        got[k] = lax.ppermute(x, axis, mirrored(axis, k))
    for k in range(0, count, 2):
        got[k + 1] = lax.ppermute(got[k], axis, mirrored(axis, 1))
    return [got[k] for k in range(count)]


def shards(cache_keys, cache_values, slot_req, slot_fill, mig_src, mig_dst, queries, new_keys, new_values, out_weight):
    slots, page, kv_local, head_dim = cache_keys.shape
    steps, requests, heads, _ = queries.shape
    peers, sides = lax.axis_size("inst"), lax.axis_size("head")
    if steps % peers or sides != 4 or peers & (peers - 1) or slots > 256:
        return general(
            cache_keys, cache_values, slot_req, slot_fill, mig_src, mig_dst, queries, new_keys, new_values, out_weight
        )
    near = steps // peers
    me = lax.axis_index("inst")
    mine = me.reshape(1).astype(jnp.int32)
    side = lax.axis_index("head").reshape(1).astype(jnp.int32)
    rows = page * kv_local
    capacity = mig_src.shape[2]
    keys = cache_keys.reshape(slots, rows, head_dim)
    values = cache_values.reshape(slots, rows, head_dim)
    outgoing, landing = mig_src.reshape(-1), mig_dst.reshape(-1)
    parcel = pack(keys, values, outgoing, landing, peers)
    parts, copied_keys, copied_values = local_attention(keys, values, slot_req, slot_fill, queries, kv_local, peers)
    parts = lax.all_to_all(parts, "inst", split_axis=0, concat_axis=0, tiled=True)
    own = lax.dynamic_slice_in_dim(queries, me * near, near, 0)
    fresh, fresh_lse = fresh_part(own, new_keys, new_values, mine, kv_local)
    parcel, fresh_lse = lax.optimization_barrier((parcel, fresh_lse))
    blocks = gather_over(combine(parts, fresh, fresh_lse, kv_local), "inst")
    parcel, _ = lax.optimization_barrier((parcel, blocks[2::2]))
    arrived = lax.all_to_all(parcel, "inst", split_axis=0, concat_axis=0, tiled=True)
    target = arrived[:, 2 * capacity * rows, :capacity].astype(jnp.int32).reshape(-1)
    moved_keys, moved_values = place(copied_keys, copied_values, arrived, outgoing, target)
    shares = project(blocks, out_weight, side, sides)
    lent = lax.ppermute(jnp.stack([shares[1], shares[3]]), "head", mirrored("head", 1))
    kept = shares[0].astype(f32) + lent[0].astype(f32)
    passed = (shares[2].astype(f32) + lent[1].astype(f32)).astype(bf16)
    total = kept + lax.ppermute(passed, "head", mirrored("head", 2)).astype(f32)
    total = total.astype(bf16).reshape(peers, near, requests, -1)
    output = jnp.take(total, jnp.arange(peers) ^ me, axis=0).reshape(steps, requests, -1)
    return moved_keys.reshape(cache_keys.shape), moved_values.reshape(cache_values.shape), output


def solution(mesh):
    in_specs = (
        P("inst", None, "head", None),
        P("inst", None, "head", None),
        P("inst"),
        P("inst"),
        P("inst", None, None),
        P("inst", None, None),
        P(None, None, "head", None),
        P(None, None, "head", None),
        P(None, None, "head", None),
        P("head", "inst"),
    )
    out_specs = (
        P("inst", None, "head", None),
        P("inst", None, "head", None),
        P(None, None, ("inst", "head")),
    )
    return jax.shard_map(shards, mesh=mesh, in_specs=in_specs, out_specs=out_specs, check_vma=False)
```
